32 devices in a mesh: grp: 4 (over y, x), blk: 8 (over z, core).
Axes of the slice: x: 2, y: 2, z: 4, core: 2. Of those that a mesh axis runs over, the one named last changes fastest.
Arguments:
- heads: bfloat16 [4096, 512], P(('grp', 'blk')), may hold values from -1.5 to 1.5
- tails: bfloat16 [65536, 512], P(('grp', 'blk')), may hold values from -1.5 to 1.5
- relation: bfloat16 [2304, 512], replicated, may hold values from -5 to 5
- head_block: int32 [8192], P(('grp', 'blk')), may hold values from 0 to 7
- tail_block: int32 [8192], P(('grp', 'blk')), may hold values from 0 to 15
- relation_id: int32 [8192], P(('grp', 'blk')), may hold values from 0 to 2303
- counts: int32 [8192, 128, 128], P(('grp', 'blk')), may hold values from 0 to 3
- owner: int32 [512, 1], P(('grp', 'blk')), may hold values from 0 to 3; in each aligned block of 16 rows (0 to 15, 16 to 31, ...) at most 8 rows name the same one
Outputs:
- head_grad: float32 [4096, 512], P(('grp', 'blk'))
- tail_grad: float32 [65536, 512], P(('grp', 'blk'))
The draws below stay inside these ranges and needn't reach their ends.
Inputs may be any that keep to these rules, and one draw needn't show every extreme that they name: `owner`: among the 16 rows of one device no group is named more than 8 times.
All inputs are finite; a program needn't handle non-finite values.
Results may differ from the reference program's by a relative error of at most 0.0095.
Values may be sent and summed in bfloat16 or wider, within the bound.
A program may use at most 128 MiB of HBM per device.

```python
import math
import jax
import jax.numpy as jnp
import numpy as np
from jax import lax

D = 512
BS = 128
NREL = 2304
TB = 16
TILES = 256
CAP = 8
HEADS = 4096
TAILS = 65536
ALL_TILES = 8192
ALL_BLOCKS = 512
N_GRP = 4
N_BLK = 8


def touch_ends(array, stream_key, smallest, largest):
    longest = array.shape.index(max(array.shape))
    spots = []
    for shift in (0, 1):
        where = [jax.random.randint(jax.random.fold_in(stream_key, axis), (), 0, length) for axis, length in enumerate(array.shape)]
        where[longest] = (where[longest] + shift) % array.shape[longest]
        spots.append(tuple(where))
    return array.at[spots[0]].set(smallest).at[spots[1]].set(largest)


def shard_levels(key, shape, split, low, top_value):
    level, own = 1.0, jax.random.fold_in(key, 6)
    for position, shards_of in split:
        draws = jnp.exp(jax.random.uniform(jax.random.fold_in(own, position), (shards_of,), jnp.float32, low / len(split), top_value / len(split)))
        level = level * jnp.repeat(draws, shape[position] // shards_of).reshape([-1 if axis == position else 1 for axis in range(len(shape))])
    return level


def shared_out(rng, own, number, rows, number_of, top, bound, skew):
    ranking = jax.random.permutation(rng, number_of)
    packed, common = load_shares(number_of, rows * top, bound, skew, True), load_shares(number_of, rows * top, bound, skew, False)
    places = jnp.arange(number_of)

    def named(lengths, offset_by):
        used = int((lengths > 0).sum())
        fixed = max(1, used // 4)
        moved = fixed + (places - fixed + offset_by * (used - fixed)) % max(1, number_of - fixed)
        return jnp.zeros((number_of,), jnp.int32).at[ranking[jnp.where(places < fixed, places, moved)]].set(jnp.asarray(lengths, jnp.int32))

    lengths = jnp.where(number % 4 == 0, named(packed, number // 4), named(common, number - number // 4 - 1))
    mixed = jax.random.permutation(jax.random.fold_in(own, 3), number_of)
    source_of, receiver = mixed[0:number_of // 2 * 2:2], mixed[1:number_of // 2 * 2:2]
    slack = jnp.minimum(lengths[source_of] - 1, bound - lengths[receiver]) // 2
    slack = jnp.where((source_of == ranking[0]) | (receiver == ranking[0]) | (lengths[receiver] == 0), 0, jnp.maximum(slack, 0))
    moved = jax.random.randint(jax.random.fold_in(own, 4), (number_of // 2,), 0, 1 << 20) % (slack + 1)
    lengths = lengths.at[source_of].add(-moved).at[receiver].add(moved)
    items = jnp.searchsorted(jnp.cumsum(lengths), jnp.arange(rows * top), side="right").astype(jnp.int32)
    listing = items.reshape(top, rows).T
    listing = listing[jax.random.permutation(jax.random.fold_in(own, 1), rows)]
    offset_by = jax.random.randint(jax.random.fold_in(own, 2), (rows, 1), 0, top)
    return jnp.take_along_axis(listing, (jnp.arange(top)[None, :] + offset_by) % top, axis=1)


def load_shares(count, total, most, skew, full):
    portions = [(1 << 20) // math.isqrt(grade ** skew) + 1 for grade in range(1, count + 1)]
    largest = most if full else min(most, max(-(-total // count), total * portions[0] // sum(portions)))
    least = 1 if total - largest >= count - 1 else 0
    holding, rest = [largest] + [least] * (count - 1), total - largest - least * (count - 1)
    while rest > 0:
        candidates = [i for i in range(1, count) if holding[i] < largest] or [i for i in range(1, count) if holding[i] < most]
        mass, left = sum([portions[i] for i in candidates]), rest
        for i in candidates:
            addition = min(most - holding[i], max(1, left * portions[i] // mass), rest)
            holding[i] = holding[i] + addition
            rest = rest - addition
    return np.array(holding)


def noise(own_key, extent, scale, reach, shards=(), kind=jnp.bfloat16):
    values = jax.random.normal(own_key, extent, jnp.float32) * scale
    if len(shards) > 0:
        values = shard_levels(own_key, extent, shards, -0.22, 0.18) * values
    return jnp.clip(values, min=-reach, max=reach).astype(kind)


def setup_inputs(seed: int = 0) -> dict:
    keys = jax.random.split(jax.random.key(seed), 9)
    heads = noise(keys[0], (HEADS, D), 0.21, 1.5, ((0, 32),))
    tails = noise(keys[1], (TAILS, D), 0.21, 1.5, ((0, 32),))
    relation = noise(keys[2], (NREL, D), 1.0, 5.0)
    head_block = touch_ends(jax.random.randint(keys[3], (ALL_TILES,), 0, N_BLK), jax.random.fold_in(keys[3], 1), 0, N_BLK - 1).astype(jnp.int32)
    tail_block = touch_ends(jax.random.randint(keys[4], (ALL_TILES,), 0, TB), jax.random.fold_in(keys[4], 1), 0, TB - 1).astype(jnp.int32)
    relation_id = touch_ends(jax.random.randint(keys[5], (ALL_TILES,), 0, NREL), jax.random.fold_in(keys[5], 1), 0, NREL - 1).astype(jnp.int32)
    counts = touch_ends(jax.random.randint(keys[6], (ALL_TILES, BS, BS), 0, 4), jax.random.fold_in(keys[6], 1), 0, 3).astype(jnp.int32)
    owner_keys = jax.random.split(jax.random.fold_in(keys[7], 1), ALL_BLOCKS // TB)
    owner_turns = jax.random.permutation(jax.random.fold_in(keys[7], 3), ALL_BLOCKS // TB)
    owner = jax.vmap(lambda own, number: shared_out(jax.random.fold_in(keys[7], 2), own, number, TB, N_GRP, 1, CAP, 2))(owner_keys, owner_turns).reshape((ALL_BLOCKS, 1))
    return {"heads": heads, "tails": tails, "relation": relation, "head_block": head_block, "tail_block": tail_block, "relation_id": relation_id, "counts": counts, "owner": owner}


grad_scale = 0.125


def local_pass(gathered, tails_local, relation, head_block, tail_block, relation_id, counts):
    tiles = head_block.shape[0]
    batch = min(16, tiles)
    turns = tiles // batch
    half = gathered.shape[2] // 2
    items = (head_block.reshape(turns, batch), tail_block.reshape(turns, batch),
             relation_id.reshape(turns, batch), counts.reshape(turns, batch, counts.shape[1], counts.shape[2]))

    def advance(carry, item):
        tail_acc, head_acc = carry
        hbk, tbk, rid, cnt = item
        hblock = gathered[hbk].astype(jnp.float32)
        tblock = tails_local[tbk]
        rel = relation[rid].astype(jnp.float32)[:, None, :]
        h_re, h_im = hblock[..., :half], hblock[..., half:]
        r_re, r_im = rel[..., :half], rel[..., half:]
        query = jnp.concatenate([h_re * r_re - h_im * r_im, h_re * r_im + h_im * r_re], axis=-1).astype(jnp.bfloat16)
        scores = jnp.einsum('kid,kjd->kij', query.astype(jnp.float32), tblock.astype(jnp.float32))
        weight = cnt.astype(jnp.float32)
        slope = (grad_scale * (jax.nn.sigmoid(scores) - weight * jax.nn.sigmoid(-scores))).astype(jnp.bfloat16)
        dtail = jnp.einsum('kij,kid->kjd', slope.astype(jnp.float32), query.astype(jnp.float32))
        dquery = jnp.einsum('kij,kjd->kid', slope.astype(jnp.float32), tblock.astype(jnp.float32))
        q_re, q_im = dquery[..., :half], dquery[..., half:]
        dhead = jnp.concatenate([q_re * r_re + q_im * r_im, q_im * r_re - q_re * r_im], axis=-1)
        return (tail_acc.at[tbk].add(dtail), head_acc.at[hbk].add(dhead)), None

    start = (jnp.zeros(tails_local.shape, jnp.float32), jnp.zeros(gathered.shape, jnp.float32))
    (tail_acc, head_acc), _ = lax.scan(advance, start, items)
    return tail_acc, head_acc


def reference(heads, tails, relation, head_block, tail_block, relation_id, counts, owner):
    devices = N_GRP * N_BLK
    heads4 = heads.reshape(N_GRP, N_BLK, BS, D)
    tails4 = tails.reshape(devices, TB, BS, D)
    groups = (jnp.arange(devices) // N_BLK).astype(jnp.int32)
    items = (tails4, head_block.reshape(devices, TILES), tail_block.reshape(devices, TILES),
             relation_id.reshape(devices, TILES), counts.reshape(devices, TILES, BS, BS), groups)

    def device_step(head_total, item):
        tails_local, hbk, tbk, rid, cnt, group = item
        gathered = lax.dynamic_index_in_dim(heads4, group, 0, keepdims=False)
        tail_acc, head_acc = local_pass(gathered, tails_local, relation, hbk, tbk, rid, cnt)
        head_low = lax.optimization_barrier(head_acc.astype(jnp.bfloat16))
        head_total = head_total.at[group].add(head_low.astype(jnp.float32))
        return head_total, tail_acc.astype(jnp.bfloat16)

    head_total, tail_local = lax.scan(device_step, jnp.zeros((N_GRP, N_BLK, BS, D), jnp.float32), items)
    tail_local = tail_local.reshape(N_GRP, N_BLK, TB, BS, D).astype(jnp.float32)
    route = owner.reshape(N_GRP, N_BLK, TB)
    onehot = (route[..., None] == jnp.arange(N_GRP, dtype=jnp.int32)).astype(jnp.float32)
    tail_grad = jnp.einsum('gbth,gbtid->hbtid', onehot, tail_local)
    return head_total.reshape(N_GRP * N_BLK * BS, D), tail_grad.reshape(N_GRP * N_BLK * TB * BS, D)
```

```python
import functools

import jax
import jax.numpy as jnp
from jax import lax
from jax.experimental import pallas as pl
from jax.experimental.pallas import tpu as pltpu
from jax.sharding import PartitionSpec as P

grad_scale = 0.125
GROUP = 4
DEPTH = 4
CHUNKS = 4


def group_lists(names, kinds, size):
    tiles = names.shape[0]
    k = jnp.arange(tiles, dtype=jnp.int32)
    same = names[:, None] == names[None, :]
    place = jnp.sum((same & (k[None, :] < k[:, None])).astype(jnp.int32), axis=1)
    t = jnp.arange(kinds + 1, dtype=jnp.int32)
    number = jnp.sum((names[None, :] == t[:, None]).astype(jnp.int32), axis=1)
    groups = (number + size - 1) // size
    start = jnp.sum(jnp.where(t[None, :] < t[:, None], groups[None, :], 0), axis=1)
    base = jnp.sum(jnp.where(names[:, None] == t[None, :], start[None, :], 0), axis=1)
    spot = base * size + place
    total = (tiles // size + kinds) * size
    p = jnp.arange(total, dtype=jnp.int32)
    listing = jnp.sum(jnp.where(spot[None, :] == p[:, None], k[None, :] + 1, 0), axis=1) - 1
    return listing, start


def tail_kernel(first, list_ref, gs_ref, hb_ref, heads_ref, tails_ref, rel_ref, counts_ref, *rest):
    tail_out, slope_out, cbuf, sbuf, acc, csem, ssem = rest[-7:]
    own = tails_ref.shape[0]
    half = tails_ref.shape[2] // 2
    begin = gs_ref[first]
    end = gs_ref[first + own]

    def fetch(j, slot):
        for g in range(GROUP):
            k = jnp.maximum(list_ref[j * GROUP + g], 0)
            pltpu.make_async_copy(counts_ref.at[k], cbuf.at[slot, g], csem.at[slot, g]).start()

    def settle(slot):
        for g in range(GROUP):
            pltpu.make_async_copy(sbuf.at[slot, g], slope_out.at[0], ssem.at[slot, g]).wait()

    for d in range(DEPTH - 1):
        @pl.when(begin + d < end)
        def _():
            fetch(begin + d, d)

    def body(t, j):
        step = j - begin
        slot = lax.rem(step, DEPTH)
        out = lax.rem(step, 2)
        ahead = j + DEPTH - 1

        @pl.when(ahead < end)
        def _():
            fetch(ahead, lax.rem(step + DEPTH - 1, DEPTH))

        @pl.when(step >= 2)
        def _():
            settle(out)

        for g in range(GROUP):
            pltpu.make_async_copy(counts_ref.at[0], cbuf.at[slot, g], csem.at[slot, g]).wait()
        tail = tails_ref[t]
        queries, slopes = [], []
        for g in range(GROUP):
            entry = list_ref[j * GROUP + g]
            k = jnp.maximum(entry, 0)
            scale = jnp.where(entry >= 0, 0.5 * grad_scale, 0.0).astype(jnp.float32)
            h = heads_ref[hb_ref[k]]
            r = rel_ref[pl.ds(k, 1), :].astype(jnp.bfloat16)
            h_re, h_im = h[:, :half], h[:, half:]
            r_re, r_im = r[:, :half], r[:, half:]
            q = jnp.concatenate([h_re * r_re - h_im * r_im, h_re * r_im + h_im * r_re], axis=1)
            s = lax.dot_general(q, tail, (((1,), (1,)), ((), ())), preferred_element_type=jnp.float32)
            w = cbuf[slot, g].astype(jnp.float32) * scale
            slope = ((scale - w) + jnp.tanh(0.5 * s) * (scale + w)).astype(jnp.bfloat16)
            sbuf[out, g] = slope
            queries.append(q)
            slopes.append(slope)
        acc[...] += lax.dot_general(
            jnp.concatenate(slopes, axis=0),
            jnp.concatenate(queries, axis=0),
            (((0,), (0,)), ((), ())),
            preferred_element_type=jnp.float32,
        )
        for g in range(GROUP):
            entry = list_ref[j * GROUP + g]
            k = jnp.where(entry >= 0, entry, slope_out.shape[0] - 1)
            pltpu.make_async_copy(sbuf.at[out, g], slope_out.at[k], ssem.at[out, g]).start()

    def per_tail(t, carry):
        acc[...] = jnp.zeros_like(acc)

        def inner(j, c):
            body(t, j)
            return c

        lax.fori_loop(gs_ref[first + t], gs_ref[first + t + 1], inner, 0)
        tail_out[t] = acc[...].astype(jnp.bfloat16)
        return carry

    lax.fori_loop(0, own, per_tail, 0)
    steps = end - begin
    for back in (2, 1):
        @pl.when(steps >= back)
        def _():
            settle(lax.rem(steps - back, 2))


def head_kernel(list_ref, gs_ref, tb_ref, tails_ref, rel_ref, slope_ref, head_out, buf, acc, sem):
    members = head_out.shape[0]
    half = tails_ref.shape[2] // 2
    end = gs_ref[members]

    def fetch(j, slot):
        for g in range(GROUP):
            k = jnp.maximum(list_ref[j * GROUP + g], 0)
            pltpu.make_async_copy(slope_ref.at[k], buf.at[slot, g], sem.at[slot, g]).start()

    for d in range(DEPTH - 1):
        @pl.when(d < end)
        def _():
            fetch(d, d)

    def body(j):
        slot = lax.rem(j, DEPTH)

        @pl.when(j + DEPTH - 1 < end)
        def _():
            fetch(j + DEPTH - 1, lax.rem(j + DEPTH - 1, DEPTH))

        for g in range(GROUP):
            pltpu.make_async_copy(slope_ref.at[0], buf.at[slot, g], sem.at[slot, g]).wait()
        turned, slopes = [], []
        for g in range(GROUP):
            entry = list_ref[j * GROUP + g]
            k = jnp.maximum(entry, 0)
            t = tails_ref[tb_ref[k]]
            keep = jnp.where(entry >= 0, 1.0, 0.0).astype(jnp.float32)
            r = (rel_ref[pl.ds(k, 1), :] * keep).astype(jnp.bfloat16)
            t_re, t_im = t[:, :half], t[:, half:]
            r_re, r_im = r[:, :half], r[:, half:]
            turned.append(
                jnp.concatenate([t_re * r_re + t_im * r_im, t_im * r_re - t_re * r_im], axis=1)
            )
            slopes.append(buf[slot, g])
        acc[...] += jnp.dot(
            jnp.concatenate(slopes, axis=1),
            jnp.concatenate(turned, axis=0),
            preferred_element_type=jnp.float32,
        )

    def per_head(h, carry):
        acc[...] = jnp.zeros_like(acc)

        def inner(j, c):
            body(j)
            return c

        lax.fori_loop(gs_ref[h], gs_ref[h + 1], inner, 0)
        head_out[h] = acc[...].astype(jnp.bfloat16)
        return carry

    lax.fori_loop(0, members, per_head, 0)


smem = pl.BlockSpec(memory_space=pltpu.SMEM)
vmem = pl.BlockSpec(memory_space=pltpu.VMEM)
hbm = pl.BlockSpec(memory_space=pl.ANY)


def tail_chunk(first, own, listing, starts, hb, heads, tails, rel, counts, slopes):
    tiles, rows, _ = counts.shape
    width = tails.shape[2]
    work = tiles * own // 16
    args = [listing, starts, hb, heads, tails, rel, counts]
    specs = [smem, smem, smem, vmem, vmem, vmem, hbm]
    aliases = {}
    if slopes is not None:
        args.append(slopes)
        specs.append(hbm)
        aliases = {len(args) - 1: 1}
    return pl.pallas_call(
        functools.partial(tail_kernel, first),
        out_shape=[
            jax.ShapeDtypeStruct((own, rows, width), jnp.bfloat16),
            jax.ShapeDtypeStruct((tiles + 1, rows, rows), jnp.bfloat16),
        ],
        in_specs=specs,
        out_specs=[vmem, hbm],
        scratch_shapes=[
            pltpu.VMEM((DEPTH, GROUP, rows, rows), jnp.int32),
            pltpu.VMEM((2, GROUP, rows, rows), jnp.bfloat16),
            pltpu.VMEM((rows, width), jnp.float32),
            pltpu.SemaphoreType.DMA((DEPTH, GROUP)),
            pltpu.SemaphoreType.DMA((2, GROUP)),
        ],
        input_output_aliases=aliases,
        compiler_params=pltpu.CompilerParams(vmem_limit_bytes=32 * 1024 * 1024),
        cost_estimate=pl.CostEstimate(
            flops=8 * work * rows * rows * width,
            bytes_accessed=work * rows * rows * 6,
            transcendentals=work * rows * rows,
        ),
        name="tail_chunk",
    )(*args)


def head_pass(members, listing, starts, tb, tails, rel, slopes):
    _, rows, width = tails.shape
    work = slopes.shape[0]
    return pl.pallas_call(
        head_kernel,
        out_shape=jax.ShapeDtypeStruct((members, rows, width), jnp.bfloat16),
        in_specs=[smem, smem, smem, vmem, vmem, hbm],
        out_specs=vmem,
        scratch_shapes=[
            pltpu.VMEM((DEPTH, GROUP, rows, rows), jnp.bfloat16),
            pltpu.VMEM((rows, width), jnp.float32),
            pltpu.SemaphoreType.DMA((DEPTH, GROUP)),
        ],
        compiler_params=pltpu.CompilerParams(vmem_limit_bytes=32 * 1024 * 1024),
        cost_estimate=pl.CostEstimate(
            flops=4 * work * rows * rows * width,
            bytes_accessed=work * rows * rows * 2,
            transcendentals=0,
        ),
        name="head_pass",
    )(listing, starts, tb, tails, rel, slopes)


def on_device(heads, tails, relation, head_block, tail_block, relation_id, counts, owner):
    rows, width = heads.shape
    members = lax.axis_size("blk")
    groups = lax.axis_size("grp")
    blocks = tails.shape[0] // rows
    me = lax.axis_index("grp")
    gathered = lax.all_gather(heads, "blk", axis=0, tiled=True).reshape(members, rows, width)
    owners = lax.all_gather(owner[:, 0], "grp", axis=0)
    tails3 = tails.reshape(blocks, rows, width)
    kinds = jnp.arange(relation.shape[0], dtype=jnp.int32)
    pick = (relation_id[:, None] == kinds[None, :]).astype(jnp.bfloat16)
    rel = jnp.dot(pick, relation, preferred_element_type=jnp.float32)
    by_tail, tail_starts = group_lists(tail_block, blocks, GROUP)
    by_head, head_starts = group_lists(head_block, members, GROUP)

    own = blocks // CHUNKS
    slopes = None
    parts = []
    for c in range(CHUNKS):
        part, slopes = tail_chunk(
            c * own, own, by_tail, tail_starts, head_block, gathered,
            tails3[c * own : (c + 1) * own], rel, counts, slopes,
        )
        parts.append(part)

    head_local = head_pass(members, by_head, head_starts, tail_block, tails3, rel, slopes)
    head_grad = lax.psum_scatter(
        head_local.reshape(members * rows, width), "blk", scatter_dimension=0, tiled=True
    ).astype(jnp.float32)

    def named(source, target, at, count):
        route = lax.dynamic_slice_in_dim(
            lax.dynamic_index_in_dim(owners, source, 0, keepdims=False), at, count
        )
        return (route == target)[:, None, None]

    def take(mask, value):
        return jnp.where(mask, value.astype(jnp.float32), 0.0)

    piece = own // 2
    outs = []
    for c in range(CHUNKS):
        for side in range(2):
            near, far = (1, 2) if side == 0 else (2, 1)
            at = c * own + side * piece
            mine = parts[c][side * piece : (side + 1) * piece]
            theirs = lax.ppermute(mine, "grp", [(g, g ^ near) for g in range(groups)])
            onward = (
                take(named(me, me ^ far, at, piece), mine)
                + take(named(me ^ near, me ^ far, at, piece), theirs)
            ).astype(jnp.bfloat16)
            last = lax.ppermute(onward, "grp", [(g, g ^ far) for g in range(groups)])
            outs.append(
                take(named(me, me, at, piece), mine)
                + take(named(me ^ near, me, at, piece), theirs)
                + last.astype(jnp.float32)
            )
    tail_grad = jnp.concatenate(outs, axis=0).reshape(blocks * rows, width)
    return (head_grad, tail_grad)


def solution(mesh):
    placed = (
        P(("grp", "blk"), None),
        P(("grp", "blk"), None),
        P(),
        P(("grp", "blk")),
        P(("grp", "blk")),
        P(("grp", "blk")),
        P(("grp", "blk"), None, None),
        P(("grp", "blk"), None),
    )
    return jax.shard_map(
        on_device,
        mesh=mesh,
        in_specs=placed,
        out_specs=(P(("grp", "blk"), None), P(("grp", "blk"), None)),
        check_vma=False,
    )
```

```python
import functools

import jax
import jax.numpy as jnp
from jax import lax
from jax.experimental import pallas as pl
from jax.experimental.pallas import tpu as pltpu
from jax.sharding import PartitionSpec as P

grad_scale = 0.125
GROUP = 8
DEPTH = 4
CHUNKS = 2


def group_lists(names, kinds, size):
    tiles = names.shape[0]
    k = jnp.arange(tiles, dtype=jnp.int32)
    same = names[:, None] == names[None, :]
    place = jnp.sum((same & (k[None, :] < k[:, None])).astype(jnp.int32), axis=1)
    t = jnp.arange(kinds + 1, dtype=jnp.int32)
    number = jnp.sum((names[None, :] == t[:, None]).astype(jnp.int32), axis=1)
    groups = (number + size - 1) // size
    start = jnp.sum(jnp.where(t[None, :] < t[:, None], groups[None, :], 0), axis=1)
    base = jnp.sum(jnp.where(names[:, None] == t[None, :], start[None, :], 0), axis=1)
    spot = base * size + place
    total = (tiles // size + kinds) * size
    p = jnp.arange(total, dtype=jnp.int32)
    listing = jnp.sum(jnp.where(spot[None, :] == p[:, None], k[None, :] + 1, 0), axis=1) - 1
    return listing, start


def tail_kernel(first, list_ref, gs_ref, hb_ref, heads_ref, tails_ref, rel_ref, counts_ref, *rest):
    tail_out, slope_out, cbuf, sbuf, acc, csem, ssem = rest[-7:]
    own = tails_ref.shape[0]
    half = tails_ref.shape[2] // 2
    begin = gs_ref[first]
    end = gs_ref[first + own]

    def fetch(j, slot):
        for g in range(GROUP):
            k = jnp.maximum(list_ref[j * GROUP + g], 0)
            pltpu.make_async_copy(counts_ref.at[k], cbuf.at[slot, g], csem.at[slot, g]).start()

    def settle(slot):
        for g in range(GROUP):
            pltpu.make_async_copy(sbuf.at[slot, g], slope_out.at[0], ssem.at[slot, g]).wait()

    for d in range(DEPTH - 1):
        @pl.when(begin + d < end)
        def _():
            fetch(begin + d, d)

    def body(t, j):
        step = j - begin
        slot = lax.rem(step, DEPTH)
        out = lax.rem(step, 2)
        ahead = j + DEPTH - 1

        @pl.when(ahead < end)
        def _():
            fetch(ahead, lax.rem(step + DEPTH - 1, DEPTH))

        @pl.when(step >= 2)
        def _():
            settle(out)

        for g in range(GROUP):
            pltpu.make_async_copy(counts_ref.at[0], cbuf.at[slot, g], csem.at[slot, g]).wait()
        tail = tails_ref[t]
        queries, slopes = [], []
        for g in range(GROUP):
            entry = list_ref[j * GROUP + g]
            k = jnp.maximum(entry, 0)
            scale = jnp.where(entry >= 0, 0.5 * grad_scale, 0.0).astype(jnp.float32)
            h = heads_ref[hb_ref[k]]
            r = rel_ref[pl.ds(k, 1), :].astype(jnp.bfloat16)
            h_re, h_im = h[:, :half], h[:, half:]
            r_re, r_im = r[:, :half], r[:, half:]
            q = jnp.concatenate([h_re * r_re - h_im * r_im, h_re * r_im + h_im * r_re], axis=1)
            s = lax.dot_general(q, tail, (((1,), (1,)), ((), ())), preferred_element_type=jnp.float32)
            w = cbuf[slot, g].astype(jnp.float32) * scale
            slope = ((scale - w) + jnp.tanh(0.5 * s) * (scale + w)).astype(jnp.bfloat16)
            sbuf[out, g] = slope
            queries.append(q)
            slopes.append(slope)
        acc[...] += lax.dot_general(
            jnp.concatenate(slopes, axis=0),
            jnp.concatenate(queries, axis=0),
            (((0,), (0,)), ((), ())),
            preferred_element_type=jnp.float32,
        )
        for g in range(GROUP):
            entry = list_ref[j * GROUP + g]
            k = jnp.where(entry >= 0, entry, slope_out.shape[0] - 1)
            pltpu.make_async_copy(sbuf.at[out, g], slope_out.at[k], ssem.at[out, g]).start()

    def per_tail(t, carry):
        acc[...] = jnp.zeros_like(acc)

        def inner(j, c):
            body(t, j)
            return c

        lax.fori_loop(gs_ref[first + t], gs_ref[first + t + 1], inner, 0)
        tail_out[t] = acc[...].astype(jnp.bfloat16)
        return carry

    lax.fori_loop(0, own, per_tail, 0)
    steps = end - begin
    for back in (2, 1):
        @pl.when(steps >= back)
        def _():
            settle(lax.rem(steps - back, 2))


def head_kernel(first, list_ref, gs_ref, tb_ref, tails_ref, rel_ref, slope_ref, head_out, buf, acc, sem):
    members = head_out.shape[0]
    half = tails_ref.shape[2] // 2
    begin = gs_ref[first]
    end = gs_ref[first + members]

    def fetch(j, slot):
        for g in range(GROUP):
            k = jnp.maximum(list_ref[j * GROUP + g], 0)
            pltpu.make_async_copy(slope_ref.at[k], buf.at[slot, g], sem.at[slot, g]).start()

    for d in range(DEPTH - 1):
        @pl.when(begin + d < end)
        def _():
            fetch(begin + d, d)

    def body(j):
        step = j - begin
        slot = lax.rem(step, DEPTH)

        @pl.when(j + DEPTH - 1 < end)
        def _():
            fetch(j + DEPTH - 1, lax.rem(step + DEPTH - 1, DEPTH))

        for g in range(GROUP):
            pltpu.make_async_copy(slope_ref.at[0], buf.at[slot, g], sem.at[slot, g]).wait()
        turned, slopes = [], []
        for g in range(GROUP):
            entry = list_ref[j * GROUP + g]
            k = jnp.maximum(entry, 0)
            t = tails_ref[tb_ref[k]]
            keep = jnp.where(entry >= 0, 1.0, 0.0).astype(jnp.float32)
            r = (rel_ref[pl.ds(k, 1), :] * keep).astype(jnp.bfloat16)
            t_re, t_im = t[:, :half], t[:, half:]
            r_re, r_im = r[:, :half], r[:, half:]
            turned.append(
                jnp.concatenate([t_re * r_re + t_im * r_im, t_im * r_re - t_re * r_im], axis=1)
            )
            slopes.append(buf[slot, g])
        acc[...] += jnp.dot(
            jnp.concatenate(slopes, axis=1),
            jnp.concatenate(turned, axis=0),
            preferred_element_type=jnp.float32,
        )

    def per_head(h, carry):
        acc[...] = jnp.zeros_like(acc)

        def inner(j, c):
            body(j)
            return c

        lax.fori_loop(gs_ref[first + h], gs_ref[first + h + 1], inner, 0)
        head_out[h] = acc[...].astype(jnp.bfloat16)
        return carry

    lax.fori_loop(0, members, per_head, 0)


smem = pl.BlockSpec(memory_space=pltpu.SMEM)
vmem = pl.BlockSpec(memory_space=pltpu.VMEM)
hbm = pl.BlockSpec(memory_space=pl.ANY)


def tail_chunk(first, own, listing, starts, hb, heads, tails, rel, counts, slopes):
    tiles, rows, _ = counts.shape
    width = tails.shape[2]
    work = tiles * own // 16
    args = [listing, starts, hb, heads, tails, rel, counts]
    specs = [smem, smem, smem, vmem, vmem, vmem, hbm]
    aliases = {}
    if slopes is not None:
        args.append(slopes)
        specs.append(hbm)
        aliases = {len(args) - 1: 1}
    return pl.pallas_call(
        functools.partial(tail_kernel, first),
        out_shape=[
            jax.ShapeDtypeStruct((own, rows, width), jnp.bfloat16),
            jax.ShapeDtypeStruct((tiles + 1, rows, rows), jnp.bfloat16),
        ],
        in_specs=specs,
        out_specs=[vmem, hbm],
        scratch_shapes=[
            pltpu.VMEM((DEPTH, GROUP, rows, rows), jnp.int32),
            pltpu.VMEM((2, GROUP, rows, rows), jnp.bfloat16),
            pltpu.VMEM((rows, width), jnp.float32),
            pltpu.SemaphoreType.DMA((DEPTH, GROUP)),
            pltpu.SemaphoreType.DMA((2, GROUP)),
        ],
        input_output_aliases=aliases,
        compiler_params=pltpu.CompilerParams(vmem_limit_bytes=32 * 1024 * 1024),
        cost_estimate=pl.CostEstimate(
            flops=26 * work * rows * rows * width,
            bytes_accessed=work * rows * rows * 6,
            transcendentals=work * rows * rows,
        ),
        name="tail_chunk",
    )(*args)


def head_pass(first, members, share, listing, starts, tb, tails, rel, slopes):
    _, rows, width = tails.shape
    work = slopes.shape[0] // share
    return pl.pallas_call(
        functools.partial(head_kernel, first),
        out_shape=jax.ShapeDtypeStruct((members, rows, width), jnp.bfloat16),
        in_specs=[smem, smem, smem, vmem, vmem, hbm],
        out_specs=vmem,
        scratch_shapes=[
            pltpu.VMEM((DEPTH, GROUP, rows, rows), jnp.bfloat16),
            pltpu.VMEM((rows, width), jnp.float32),
            pltpu.SemaphoreType.DMA((DEPTH, GROUP)),
        ],
        compiler_params=pltpu.CompilerParams(vmem_limit_bytes=32 * 1024 * 1024),
        cost_estimate=pl.CostEstimate(
            flops=16 * work * rows * rows * width,
            bytes_accessed=work * rows * rows * 2,
            transcendentals=0,
        ),
        name="head_pass",
    )(listing, starts, tb, tails, rel, slopes)


def on_device(heads, tails, relation, head_block, tail_block, relation_id, counts, owner):
    rows, width = heads.shape
    members = lax.axis_size("blk")
    groups = lax.axis_size("grp")
    blocks = tails.shape[0] // rows
    me = lax.axis_index("grp")
    gathered = lax.all_gather(heads, "blk", axis=0, tiled=True).reshape(members, rows, width)
    owners = lax.all_gather(owner[:, 0], "grp", axis=0)
    tails3 = tails.reshape(blocks, rows, width)
    kinds = jnp.arange(relation.shape[0], dtype=jnp.int32)
    pick = (relation_id[:, None] == kinds[None, :]).astype(jnp.bfloat16)
    rel = jnp.dot(pick, relation, preferred_element_type=jnp.float32)
    by_tail, tail_starts = group_lists(tail_block, blocks, GROUP)
    by_head, head_starts = group_lists(head_block, members, GROUP)

    own = blocks // CHUNKS
    slopes = None
    parts = []
    for c in range(CHUNKS):
        part, slopes = tail_chunk(
            c * own, own, by_tail, tail_starts, head_block, gathered,
            tails3[c * own : (c + 1) * own], rel, counts, slopes,
        )
        parts.append(part)

    def named(source, target, at, count):
        route = lax.dynamic_slice_in_dim(
            lax.dynamic_index_in_dim(owners, source, 0, keepdims=False), at, count
        )
        return (route == target)[:, None, None]

    def take(mask, value):
        return jnp.where(mask, value.astype(jnp.float32), 0.0)

    piece = own // 2
    kept, onwards = [], []
    for c in range(CHUNKS):
        for side in range(2):
            near, far = (1, 2) if side == 0 else (2, 1)
            at = c * own + side * piece
            mine = parts[c][side * piece : (side + 1) * piece]
            theirs = lax.ppermute(mine, "grp", [(g, g ^ near) for g in range(groups)])
            onwards.append(
                (
                    take(named(me, me ^ far, at, piece), mine)
                    + take(named(me ^ near, me ^ far, at, piece), theirs)
                ).astype(jnp.bfloat16)
            )
            kept.append((near, far, at, mine, theirs))

    def onward_step(i, value):
        far = kept[i][1]
        return lax.ppermute(value, "grp", [(g, g ^ far) for g in range(groups)])

    early = 2 * (CHUNKS - 1)
    part = members // 2
    slopes, *onwards[:early] = lax.optimization_barrier((slopes, *onwards[:early]))
    lasts = [onward_step(i, v) for i, v in enumerate(onwards[:early])]
    low = head_pass(0, part, 2, by_head, head_starts, tail_block, tails3, rel, slopes)
    slopes, low, lasts, onwards = lax.optimization_barrier((slopes, low, lasts, onwards))
    lasts = lasts + [onward_step(i, onwards[i]) for i in range(early, len(onwards))]
    high = head_pass(
        part, members - part, 2, by_head, head_starts, tail_block, tails3, rel, slopes
    )
    head_local = jnp.concatenate([low, high], axis=0)
    head_grad = lax.psum_scatter(
        head_local.reshape(members * rows, width), "blk", scatter_dimension=0, tiled=True
    ).astype(jnp.float32)

    outs = []
    for last, (near, far, at, mine, theirs) in zip(lasts, kept):
        outs.append(
            take(named(me, me, at, piece), mine)
            + take(named(me ^ near, me, at, piece), theirs)
            + last.astype(jnp.float32)
        )
    tail_grad = jnp.concatenate(outs, axis=0).reshape(blocks * rows, width)
    return (head_grad, tail_grad)


def solution(mesh):
    placed = (
        P(("grp", "blk"), None),
        P(("grp", "blk"), None),
        P(),
        P(("grp", "blk")),
        P(("grp", "blk")),
        P(("grp", "blk")),
        P(("grp", "blk"), None, None),
        P(("grp", "blk"), None),
    )
    return jax.shard_map(
        on_device,
        mesh=mesh,
        in_specs=placed,
        out_specs=(P(("grp", "blk"), None), P(("grp", "blk"), None)),
        check_vma=False,
    )
```

```python
import functools

import jax
import jax.numpy as jnp
from jax import lax
from jax.experimental import pallas as pl
from jax.experimental.pallas import tpu as pltpu
from jax.sharding import PartitionSpec as P

grad_scale = 0.125
GROUP = 8
DEPTH = 4
CHUNKS = 2


def group_lists(names, kinds, size):
    tiles = names.shape[0]
    k = jnp.arange(tiles, dtype=jnp.int32)
    same = names[:, None] == names[None, :]
    place = jnp.sum((same & (k[None, :] < k[:, None])).astype(jnp.int32), axis=1)
    t = jnp.arange(kinds + 1, dtype=jnp.int32)
    number = jnp.sum((names[None, :] == t[:, None]).astype(jnp.int32), axis=1)
    groups = (number + size - 1) // size
    start = jnp.sum(jnp.where(t[None, :] < t[:, None], groups[None, :], 0), axis=1)
    base = jnp.sum(jnp.where(names[:, None] == t[None, :], start[None, :], 0), axis=1)
    spot = base * size + place
    total = (tiles // size + kinds) * size
    p = jnp.arange(total, dtype=jnp.int32)
    listing = jnp.sum(jnp.where(spot[None, :] == p[:, None], k[None, :] + 1, 0), axis=1) - 1
    return listing, start


def tail_kernel(first, list_ref, gs_ref, hb_ref, heads_ref, tails_ref, rel_ref, counts_ref, *rest):
    tail_out, slope_out, cbuf, sbuf, acc, csem, ssem = rest[-7:]
    own = tails_ref.shape[0]
    half = tails_ref.shape[2] // 2
    begin = gs_ref[first]
    end = gs_ref[first + own]

    def fetch(j, slot):
        for g in range(GROUP):
            k = jnp.maximum(list_ref[j * GROUP + g], 0)
            pltpu.make_async_copy(counts_ref.at[k], cbuf.at[slot, g], csem.at[slot, g]).start()

    def settle(slot):
        for g in range(GROUP):
            pltpu.make_async_copy(sbuf.at[slot, g], slope_out.at[0], ssem.at[slot, g]).wait()

    for d in range(DEPTH - 1):
        @pl.when(begin + d < end)
        def _():
            fetch(begin + d, d)

    def body(t, j):
        step = j - begin
        slot = lax.rem(step, DEPTH)
        out = lax.rem(step, 2)
        ahead = j + DEPTH - 1

        @pl.when(ahead < end)
        def _():
            fetch(ahead, lax.rem(step + DEPTH - 1, DEPTH))

        @pl.when(step >= 2)
        def _():
            settle(out)

        for g in range(GROUP):
            pltpu.make_async_copy(counts_ref.at[0], cbuf.at[slot, g], csem.at[slot, g]).wait()
        tail = tails_ref[t]
        queries, slopes = [], []
        for g in range(GROUP):
            entry = list_ref[j * GROUP + g]
            k = jnp.maximum(entry, 0)
            scale = jnp.where(entry >= 0, 0.5 * grad_scale, 0.0).astype(jnp.float32)
            h = heads_ref[hb_ref[k]]
            r = rel_ref[pl.ds(k, 1), :].astype(jnp.bfloat16)
            h_re, h_im = h[:, :half], h[:, half:]
            r_re, r_im = r[:, :half], r[:, half:]
            q = jnp.concatenate([h_re * r_re - h_im * r_im, h_re * r_im + h_im * r_re], axis=1)
            s = lax.dot_general(q, tail, (((1,), (1,)), ((), ())), preferred_element_type=jnp.float32)
            w = cbuf[slot, g].astype(jnp.float32) * scale
            slope = ((scale - w) + jnp.tanh(0.5 * s) * (scale + w)).astype(jnp.bfloat16)
            sbuf[out, g] = slope
            queries.append(q)
            slopes.append(slope)
        acc[...] += lax.dot_general(
            jnp.concatenate(slopes, axis=0),
            jnp.concatenate(queries, axis=0),
            (((0,), (0,)), ((), ())),
            preferred_element_type=jnp.float32,
        )
        for g in range(GROUP):
            entry = list_ref[j * GROUP + g]
            k = jnp.where(entry >= 0, entry, slope_out.shape[0] - 1)
            pltpu.make_async_copy(sbuf.at[out, g], slope_out.at[k], ssem.at[out, g]).start()

    def per_tail(t, carry):
        acc[...] = jnp.zeros_like(acc)

        def inner(j, c):
            body(t, j)
            return c

        lax.fori_loop(gs_ref[first + t], gs_ref[first + t + 1], inner, 0)
        tail_out[t] = acc[...].astype(jnp.bfloat16)
        return carry

    lax.fori_loop(0, own, per_tail, 0)
    steps = end - begin
    for back in (2, 1):
        @pl.when(steps >= back)
        def _():
            settle(lax.rem(steps - back, 2))


def head_kernel(first, list_ref, gs_ref, tb_ref, tails_ref, rel_ref, slope_ref, head_out, buf, acc, sem):
    members = head_out.shape[0]
    half = tails_ref.shape[2] // 2
    begin = gs_ref[first]
    end = gs_ref[first + members]

    def fetch(j, slot):
        for g in range(GROUP):
            k = jnp.maximum(list_ref[j * GROUP + g], 0)
            pltpu.make_async_copy(slope_ref.at[k], buf.at[slot, g], sem.at[slot, g]).start()

    for d in range(DEPTH - 1):
        @pl.when(begin + d < end)
        def _():
            fetch(begin + d, d)

    def body(j):
        step = j - begin
        slot = lax.rem(step, DEPTH)

        @pl.when(j + DEPTH - 1 < end)
        def _():
            fetch(j + DEPTH - 1, lax.rem(step + DEPTH - 1, DEPTH))

        for g in range(GROUP):
            pltpu.make_async_copy(slope_ref.at[0], buf.at[slot, g], sem.at[slot, g]).wait()
        turned, slopes = [], []
        for g in range(GROUP):
            entry = list_ref[j * GROUP + g]
            k = jnp.maximum(entry, 0)
            t = tails_ref[tb_ref[k]]
            keep = jnp.where(entry >= 0, 1.0, 0.0).astype(jnp.float32)
            r = (rel_ref[pl.ds(k, 1), :] * keep).astype(jnp.bfloat16)
            t_re, t_im = t[:, :half], t[:, half:]
            r_re, r_im = r[:, :half], r[:, half:]
            turned.append(
                jnp.concatenate([t_re * r_re + t_im * r_im, t_im * r_re - t_re * r_im], axis=1)
            )
            slopes.append(buf[slot, g])
        acc[...] += jnp.dot(
            jnp.concatenate(slopes, axis=1),
            jnp.concatenate(turned, axis=0),
            preferred_element_type=jnp.float32,
        )

    def per_head(h, carry):
        acc[...] = jnp.zeros_like(acc)

        def inner(j, c):
            body(j)
            return c

        lax.fori_loop(gs_ref[first + h], gs_ref[first + h + 1], inner, 0)
        head_out[h] = acc[...].astype(jnp.bfloat16)
        return carry

    lax.fori_loop(0, members, per_head, 0)


smem = pl.BlockSpec(memory_space=pltpu.SMEM)
vmem = pl.BlockSpec(memory_space=pltpu.VMEM)
hbm = pl.BlockSpec(memory_space=pl.ANY)


def tail_chunk(first, own, listing, starts, hb, heads, tails, rel, counts, slopes):
    tiles, rows, _ = counts.shape
    width = tails.shape[2]
    work = tiles * own // 16
    args = [listing, starts, hb, heads, tails, rel, counts]
    specs = [smem, smem, smem, vmem, vmem, vmem, hbm]
    aliases = {}
    if slopes is not None:
        args.append(slopes)
        specs.append(hbm)
        aliases = {len(args) - 1: 1}
    return pl.pallas_call(
        functools.partial(tail_kernel, first),
        out_shape=[
            jax.ShapeDtypeStruct((own, rows, width), jnp.bfloat16),
            jax.ShapeDtypeStruct((tiles + 1, rows, rows), jnp.bfloat16),
        ],
        in_specs=specs,
        out_specs=[vmem, hbm],
        scratch_shapes=[
            pltpu.VMEM((DEPTH, GROUP, rows, rows), jnp.int32),
            pltpu.VMEM((2, GROUP, rows, rows), jnp.bfloat16),
            pltpu.VMEM((rows, width), jnp.float32),
            pltpu.SemaphoreType.DMA((DEPTH, GROUP)),
            pltpu.SemaphoreType.DMA((2, GROUP)),
        ],
        input_output_aliases=aliases,
        compiler_params=pltpu.CompilerParams(vmem_limit_bytes=32 * 1024 * 1024),
        cost_estimate=pl.CostEstimate(
            flops=26 * work * rows * rows * width,
            bytes_accessed=work * rows * rows * 6,
            transcendentals=work * rows * rows,
        ),
        name="tail_chunk",
    )(*args)


def head_pass(first, members, share, listing, starts, tb, tails, rel, slopes):
    _, rows, width = tails.shape
    work = slopes.shape[0] // share
    return pl.pallas_call(
        functools.partial(head_kernel, first),
        out_shape=jax.ShapeDtypeStruct((members, rows, width), jnp.bfloat16),
        in_specs=[smem, smem, smem, vmem, vmem, hbm],
        out_specs=vmem,
        scratch_shapes=[
            pltpu.VMEM((DEPTH, GROUP, rows, rows), jnp.bfloat16),
            pltpu.VMEM((rows, width), jnp.float32),
            pltpu.SemaphoreType.DMA((DEPTH, GROUP)),
        ],
        compiler_params=pltpu.CompilerParams(vmem_limit_bytes=32 * 1024 * 1024),
        cost_estimate=pl.CostEstimate(
            flops=16 * work * rows * rows * width,
            bytes_accessed=work * rows * rows * 2,
            transcendentals=0,
        ),
        name="head_pass",
    )(listing, starts, tb, tails, rel, slopes)


def on_device(heads, tails, relation, head_block, tail_block, relation_id, counts, owner):
    rows, width = heads.shape
    members = lax.axis_size("blk")
    groups = lax.axis_size("grp")
    blocks = tails.shape[0] // rows
    me = lax.axis_index("grp")
    gathered = lax.all_gather(heads, "blk", axis=0, tiled=True).reshape(members, rows, width)
    owners = lax.all_gather(owner[:, 0], "grp", axis=0)
    tails3 = tails.reshape(blocks, rows, width)
    kinds = jnp.arange(relation.shape[0], dtype=jnp.int32)
    pick = (relation_id[:, None] == kinds[None, :]).astype(jnp.bfloat16)
    rel = jnp.dot(pick, relation, preferred_element_type=jnp.float32)
    by_tail, tail_starts = group_lists(tail_block, blocks, GROUP)
    by_head, head_starts = group_lists(head_block, members, GROUP)

    own = blocks // CHUNKS
    slopes = None
    parts = []
    for c in range(CHUNKS):
        part, slopes = tail_chunk(
            c * own, own, by_tail, tail_starts, head_block, gathered,
            tails3[c * own : (c + 1) * own], rel, counts, slopes,
        )
        parts.append(part)

    def named(source, target, at, count):
        route = lax.dynamic_slice_in_dim(
            lax.dynamic_index_in_dim(owners, source, 0, keepdims=False), at, count
        )
        return (route == target)[:, None, None]

    def take(mask, value):
        return jnp.where(mask, value.astype(jnp.float32), 0.0)

    piece = own // 2
    kept, onwards = [], []
    for c in range(CHUNKS):
        for side in range(2):
            near, far = (1, 2) if side == 0 else (2, 1)
            at = c * own + side * piece
            mine = parts[c][side * piece : (side + 1) * piece]
            theirs = lax.ppermute(mine, "grp", [(g, g ^ near) for g in range(groups)])
            onwards.append(
                (
                    take(named(me, me ^ far, at, piece), mine)
                    + take(named(me ^ near, me ^ far, at, piece), theirs)
                ).astype(jnp.bfloat16)
            )
            kept.append((near, far, at, mine, theirs))

    def onward_step(i, value):
        far = kept[i][1]
        return lax.ppermute(value, "grp", [(g, g ^ far) for g in range(groups)])

    early = 2 * (CHUNKS - 1)
    part = members // 2
    slopes, *onwards[:early] = lax.optimization_barrier((slopes, *onwards[:early]))
    lasts = [onward_step(i, v) for i, v in enumerate(onwards[:early])]
    low = head_pass(0, part, 2, by_head, head_starts, tail_block, tails3, rel, slopes)
    slopes, low, onwards = lax.optimization_barrier((slopes, low, onwards))
    lasts = lasts + [onward_step(i, onwards[i]) for i in range(early, len(onwards))]
    more = (members - part) * 3 // 4
    mid = head_pass(part, more, 3, by_head, head_starts, tail_block, tails3, rel, slopes)
    slopes, mid, lasts = lax.optimization_barrier((slopes, mid, lasts))
    high = head_pass(
        part + more, members - part - more, 8, by_head, head_starts, tail_block, tails3, rel, slopes
    )
    head_local = jnp.concatenate([low, mid, high], axis=0)
    head_grad = lax.psum_scatter(
        head_local.reshape(members * rows, width), "blk", scatter_dimension=0, tiled=True
    ).astype(jnp.float32)

    outs = []
    for last, (near, far, at, mine, theirs) in zip(lasts, kept):
        outs.append(
            take(named(me, me, at, piece), mine)
            + take(named(me ^ near, me, at, piece), theirs)
            + last.astype(jnp.float32)
        )
    tail_grad = jnp.concatenate(outs, axis=0).reshape(blocks * rows, width)
    return (head_grad, tail_grad)


def solution(mesh):
    placed = (
        P(("grp", "blk"), None),
        P(("grp", "blk"), None),
        P(),
        P(("grp", "blk")),
        P(("grp", "blk")),
        P(("grp", "blk")),
        P(("grp", "blk"), None, None),
        P(("grp", "blk"), None),
    )
    return jax.shard_map(
        on_device,
        mesh=mesh,
        in_specs=placed,
        out_specs=(P(("grp", "blk"), None), P(("grp", "blk"), None)),
        check_vma=False,
    )
```
